768 devices in a mesh: row: 24 (over z, core), col: 32 (over y, x).
Axes of the slice: x: 4, y: 8, z: 12, core: 2. Of those that a mesh axis runs over, the one named last changes fastest.
Arguments:
- three_center: bfloat16 [24, 384, 131072], P(None, 'row', 'col'), may hold values from -0.0625 to 0.0625
- density: bfloat16 [131072, 1024], P('col'), may hold values from -6 to 6
- pair_mask: int32 [384, 1024], P('row', 'col'), may hold values from 0 to 1, as said below
- metric: float32 [24, 24], replicated, may hold values from -1.25 to 1.25
- aux_pairs: float32 [24, 1024, 1024], P('row', 'col'), may hold values from -0.0390625 to 0.0390625
Outputs:
- exchange_part: float32 [384, 1024], P('row')
The draws below stay inside these ranges and needn't reach their ends.
Inputs may be any that keep to these rules, and one draw needn't show every extreme that they name: `pair_mask`: in each row mu the ones form one run of consecutive atom blocks, which may start anywhere.
All inputs are finite; a program needn't handle non-finite values.
Results may differ from the reference program's by a relative error of at most 0.0003.
Values sent between devices are 32-bit elements; how exact they have to be, the bound alone decides.
No kernel may reach another device: no remote copies, remote signals or barrier semaphores. Data moves between devices by JAX's collectives and lax.ppermute only.
A program may use at most 64 MiB of HBM per device.

```python
import jax
import jax.numpy as jnp
from jax import lax

BLK = 128
MU_DEV = 16
L = 1024
PB = 24
M = 384
N = 131072
NBLK = 1024
N_ROW = 24


def draw_pair_mask(key, part):
    key = jax.random.fold_in(key, 7)
    key_len, key_pos = jax.random.split(key)
    shortest = max(1, 3 * NBLK // 100)
    longest = max(shortest + 1, NBLK // 10 + 1)
    run_len = jax.random.randint(key_len, (M, 1), shortest, longest, dtype=jnp.int32)
    spot = jax.random.randint(key_pos, (M, 1), 0, NBLK, dtype=jnp.int32)
    first = jnp.minimum(spot * spot // NBLK, NBLK - run_len)
    blocks = jnp.arange(NBLK, dtype=jnp.int32)[None, :]
    inside = jnp.logical_and(blocks >= first, blocks < first + run_len)
    return inside.astype(jnp.int32)


def block_levels(key, extent, pieces, least, top_value):
    level, own = 1.0, jax.random.fold_in(key, 6)
    for dim, shards_of in pieces:
        draws = jnp.exp(jax.random.uniform(jax.random.fold_in(own, dim), (shards_of,), jnp.float32, least / len(pieces), top_value / len(pieces)))
        level = level * jnp.repeat(draws, extent[dim] // shards_of).reshape([-1 if axis == dim else 1 for axis in range(len(extent))])
    return level


def noise(own_key, shape, width, bound, cuts=(), held_as=jnp.bfloat16):
    gain = block_levels(own_key, shape, cuts, -0.22, 0.18) if cuts else 1.0
    result = jax.random.normal(own_key, shape, jnp.float32) * width * gain
    return jnp.minimum(jnp.maximum(result, -bound), bound).astype(held_as)


def setup_inputs(seed: int = 0) -> dict:
    arg_keys = jax.random.split(jax.random.key(seed), 6)
    return {
        "three_center": noise(arg_keys[0], (PB, M, N), (N // 16) ** -0.5, 0.0625, ((1, 24), (2, 32))),
        "density": noise(arg_keys[1], (N, L), 1.0, 6.0, ((0, 32),)),
        "pair_mask": draw_pair_mask(jax.random.fold_in(arg_keys[5], 71), 0),
        "metric": noise(arg_keys[3], (PB, PB), PB ** -0.5, 1.25, (), jnp.float32),
        "aux_pairs": noise(arg_keys[4], (PB, L, L), (PB * L) ** -0.5, 0.0390625, ((0, 24), (1, 32)), jnp.float32),
    }


def reference(three_center, density, pair_mask, metric, aux_pairs):
    expand = jnp.repeat(pair_mask, BLK, axis=1).astype(jnp.bfloat16)

    def one_block(index):
        start = (index * MU_DEV).astype(jnp.int32)
        block = lax.dynamic_slice_in_dim(three_center, start, MU_DEV, 1)
        maskrows = lax.dynamic_slice_in_dim(expand, start, MU_DEV, 0)
        masked = block * maskrows[None]
        flat = masked.reshape(PB * MU_DEV, N)
        return jnp.dot(flat, density, preferred_element_type=jnp.float32).reshape(PB, MU_DEV, L)

    parts = lax.map(one_block, jnp.arange(N_ROW, dtype=jnp.int32))
    coeffs = jnp.transpose(parts, (1, 0, 2, 3)).reshape(PB, M, L)
    fitted = jnp.einsum('qp,pms->qms', metric, coeffs, precision=lax.Precision.HIGHEST)
    return jnp.einsum('qms,qsl->ml', fitted, aux_pairs, precision=lax.Precision.HIGHEST)
```

```python
import functools

import jax
import jax.numpy as jnp
from jax import lax
from jax.experimental import pallas as pl
from jax.experimental.pallas import tpu as pltpu
from jax.sharding import Mesh
from jax.sharding import PartitionSpec as P

BLK = 128
NZ, NCORE, NY, NX = 12, 2, 8, 4
NP, MU, NLOC, L = 24, 16, 4096, 1024
SIG = 32
ROWS = NP * MU
KB = 512
F32, BF16 = jnp.float32, jnp.bfloat16


def coeff_kernel(mask_ref, three_ref, dens_ref, out_ref, acc, wide):
    step = pl.program_id(0)

    @pl.when(step == 0)
    def _():
        mask = mask_ref[...].astype(F32)
        per = KB // BLK
        for b in range(NLOC // BLK):
            col = jnp.broadcast_to(mask[:, b : b + 1], (MU, BLK)).astype(BF16)
            wide[b // per, :, (b % per) * BLK : (b % per + 1) * BLK] = col

    masked = three_ref[...] * wide[step][None]
    part = jnp.dot(masked.reshape(ROWS, KB), dens_ref[...], preferred_element_type=F32)

    @pl.when(step == 0)
    def _():
        acc[...] = part

    @pl.when(step > 0)
    def _():
        acc[...] += part

    @pl.when(step == pl.num_programs(0) - 1)
    def _():
        for y in range(NY):
            turned = acc[:, y * BLK : (y + 1) * BLK].T
            for x in range(NX):
                out_ref[x, y * SIG : (y + 1) * SIG, :] = turned[x * SIG : (x + 1) * SIG]


def partial_coeffs(pair_mask, three_center, density):
    steps = NLOC // KB
    return pl.pallas_call(
        coeff_kernel,
        grid=(steps,),
        in_specs=[
            pl.BlockSpec((MU, NLOC // BLK), lambda i: (0, 0)),
            pl.BlockSpec((NP, MU, KB), lambda i: (0, 0, i)),
            pl.BlockSpec((KB, L), lambda i: (i, 0)),
        ],
        out_specs=pl.BlockSpec((NX, NY * SIG, ROWS), lambda i: (0, 0, 0)),
        out_shape=jax.ShapeDtypeStruct((NX, NY * SIG, ROWS), F32),
        scratch_shapes=[pltpu.VMEM((ROWS, L), F32), pltpu.VMEM((steps, MU, KB), BF16)],
        compiler_params=pltpu.CompilerParams(vmem_limit_bytes=58 * 1024 * 1024),
        cost_estimate=pl.CostEstimate(
            flops=2 * ROWS * NLOC * L, bytes_accessed=13_000_000, transcendentals=0
        ),
    )(pair_mask, three_center, density)


def halves(a):
    top = a.astype(BF16)
    return top, (a - top.astype(F32)).astype(BF16)


def dot3(a, b):
    a_top, a_low = halves(a)
    b_top, b_low = halves(b)
    dot = functools.partial(jnp.dot, preferred_element_type=F32)
    return dot(a_top, b_top) + (dot(a_low, b_top) + dot(a_top, b_low))


def exchange_kernel(parts_ref, mix_ref, *refs):
    aux_refs, out_ref = refs[:-1], refs[-1]
    coeffs = parts_ref[0]
    for y in range(1, NY):
        coeffs = coeffs + parts_ref[y]
    fitted = dot3(coeffs, mix_ref[...]).T
    total = None
    slots = NP // len(aux_refs)
    for g, aux_ref in enumerate(aux_refs):
        left = jnp.concatenate(
            [
                fitted[(g * slots + s) * MU : (g * slots + s + 1) * MU]
                for s in range(slots)
            ],
            axis=1,
        )
        term = dot3(left, aux_ref[...])
        total = term if total is None else total + term
    for c in range(NY * NX):
        lane, row = (c // 4) * BLK, (c % 4) * 4
        out_ref[c] = total[row : row + 4, lane : lane + BLK]


def exchange_partial(parts, mix, aux_groups):
    n = 2 + len(aux_groups)
    return pl.pallas_call(
        exchange_kernel,
        in_specs=[pl.BlockSpec(memory_space=pltpu.VMEM)] * n,
        out_specs=pl.BlockSpec(memory_space=pltpu.VMEM),
        out_shape=jax.ShapeDtypeStruct((NY * NX, 4, BLK), F32),
        compiler_params=pltpu.CompilerParams(vmem_limit_bytes=32 * 1024 * 1024),
        cost_estimate=pl.CostEstimate(
            flops=6 * MU * NP * SIG * L, bytes_accessed=4_000_000, transcendentals=0
        ),
    )(parts, mix, *aux_groups)


def shift(a, axis, size, by):
    return lax.ppermute(a, axis, [(i, (i + by) % size) for i in range(size)])


def on_device(three_center, density, pair_mask, metric, aux_pairs):
    z, core = lax.axis_index("z"), lax.axis_index("core")

    part = partial_coeffs(pair_mask, three_center, density)

    own = aux_pairs.reshape(SIG, L)
    far = jnp.concatenate(
        [own] + [shift(own, "z", NZ, by) for by in (3, 9, 6)], axis=0
    )
    groups = [far, shift(far, "z", NZ, 1), shift(far, "z", NZ, NZ - 1)]
    groups = groups + [shift(g, "core", NCORE, 1) for g in groups]
    away = jnp.array([0, -3, 3, 6], jnp.int32)
    origin = jnp.concatenate([away, away - 1, away + 1]) + z
    origin = lax.rem(origin + 2 * NZ, NZ) * NCORE
    slots = jnp.concatenate([origin + core, origin + (1 - core)])
    chosen = jnp.take(metric, slots, axis=0)
    mix = chosen.T[:, None, :, None] * jnp.eye(MU, dtype=F32)[None, :, None, :]
    mix = mix.reshape(ROWS, ROWS)

    got = lax.all_to_all(part, "x", 0, 0, tiled=True)
    mine = jnp.sum(got, axis=0).reshape(NY, SIG, ROWS)
    got = lax.all_to_all(mine, "y", 0, 0, tiled=True)
    term = exchange_partial(got, mix, groups)
    got = lax.all_to_all(term, ("y", "x"), 0, 0, tiled=True)
    done = jnp.broadcast_to(jnp.sum(got, axis=0)[None], (NY * NX, 4, BLK))
    full = lax.all_to_all(done, ("y", "x"), 0, 0, tiled=True)
    return full.reshape(8, MU, BLK).transpose(1, 0, 2).reshape(MU, L)


def solution(mesh):
    grid = Mesh(mesh.devices.reshape(NZ, NCORE, NY, NX), ("z", "core", "y", "x"))
    row, col = ("z", "core"), ("y", "x")
    placed = (P(None, row, col), P(col, None), P(row, col), P(), P(row, col, None))
    return jax.shard_map(
        on_device, mesh=grid, in_specs=placed, out_specs=P(row, None), check_vma=False
    )
```

```python
import functools

import jax
import jax.numpy as jnp
from jax import lax
from jax.experimental import pallas as pl
from jax.experimental.pallas import tpu as pltpu
from jax.sharding import Mesh
from jax.sharding import PartitionSpec as P

BLK = 128
NZ, NCORE, NY, NX = 12, 2, 8, 4
NP, MU, NLOC, L = 24, 16, 4096, 1024
SIG = 32
ROWS = NP * MU
KB = 512
AHEAD = 4
F32, BF16 = jnp.float32, jnp.bfloat16


def coeff_kernel(ahead, mask_ref, three_hbm, dens_hbm, *refs):
    out_hbm, three, dens, acc, out, three_sem, dens_sem, out_sem = refs[-8:]
    z = lax.axis_index("z")

    @pl.when((z < AHEAD) if ahead else (z >= AHEAD))
    def _():
        copies = []
        for i in range(NLOC // KB):
            part = pl.ds(i * KB, KB)
            pair = (
                pltpu.make_async_copy(three_hbm.at[:, :, part], three.at[:, :, part], three_sem.at[i]),
                pltpu.make_async_copy(dens_hbm.at[part], dens.at[part], dens_sem.at[i]),
            )
            for copy in pair:
                copy.start()
            copies.append(pair)
        mask = mask_ref[...].astype(F32)
        for i, pair in enumerate(copies):
            blocks = range(i * KB // BLK, (i + 1) * KB // BLK)
            wide = [jnp.broadcast_to(mask[:, b : b + 1], (MU, BLK)) for b in blocks]
            wide = jnp.concatenate(wide, axis=1).astype(BF16)
            for copy in pair:
                copy.wait()
            masked = (three[:, :, i * KB : (i + 1) * KB] * wide[None]).reshape(ROWS, KB)
            term = jnp.dot(masked, dens[i * KB : (i + 1) * KB, :], preferred_element_type=F32)
            if i == 0:
                acc[...] = term
            elif i < len(copies) - 1:
                acc[...] += term
            else:
                total = acc[...] + term
        backs = []
        for y in range(NY):
            rows = pl.ds(y * SIG, SIG)
            turned = total[:, y * BLK : (y + 1) * BLK].T
            out[:, y * SIG : (y + 1) * SIG, :] = turned.reshape(NX, SIG, ROWS)
            back = pltpu.make_async_copy(out.at[:, rows], out_hbm.at[:, rows], out_sem.at[y])
            back.start()
            backs.append(back)
        for back in backs:
            back.wait()


def partial_coeffs(ahead, pair_mask, three_center, density, *held):
    chunks = NLOC // KB
    anywhere = pl.BlockSpec(memory_space=pl.ANY)
    part = jax.ShapeDtypeStruct((NX, NY * SIG, ROWS), F32)
    return pl.pallas_call(
        functools.partial(coeff_kernel, ahead),
        in_specs=[pl.BlockSpec(memory_space=pltpu.VMEM)] + [anywhere] * (2 + len(held)),
        out_specs=anywhere,
        out_shape=part,
        scratch_shapes=[
            pltpu.VMEM((NP, MU, NLOC), BF16),
            pltpu.VMEM((NLOC, L), BF16),
            pltpu.VMEM((ROWS, L), F32),
            pltpu.VMEM((NX, NY * SIG, ROWS), F32),
            pltpu.SemaphoreType.DMA((chunks,)),
            pltpu.SemaphoreType.DMA((chunks,)),
            pltpu.SemaphoreType.DMA((NY,)),
        ],
        input_output_aliases={} if ahead else {3: 0},
        compiler_params=pltpu.CompilerParams(vmem_limit_bytes=56 * 1024 * 1024),
        cost_estimate=pl.CostEstimate(
            flops=2 * ROWS * NLOC * L, bytes_accessed=13_000_000, transcendentals=0
        ),
    )(pair_mask, three_center, density, *held)


def sum_kernel(got_ref, out_ref):
    for y in range(NY):
        got = got_ref[:, y * SIG : (y + 1) * SIG]
        out_ref[y] = (got[0] + got[1]) + (got[2] + got[3])


def summed(got):
    return pl.pallas_call(
        sum_kernel,
        in_specs=[pl.BlockSpec(memory_space=pltpu.VMEM)],
        out_specs=pl.BlockSpec(memory_space=pltpu.VMEM),
        out_shape=jax.ShapeDtypeStruct((NY, SIG, ROWS), F32),
        compiler_params=pltpu.CompilerParams(vmem_limit_bytes=4 * 1024 * 1024),
        cost_estimate=pl.CostEstimate(
            flops=NX * NY * SIG * ROWS, bytes_accessed=2_000_000, transcendentals=0
        ),
    )(got)


def mixing(z, core, metric):
    slot = lax.broadcasted_iota(jnp.int32, (1, ROWS), 1) // MU
    holder = jnp.where(slot < NZ, core, 1 - core)
    group, kind = (slot % NZ) // 3, slot % 3
    near = jnp.where(group == 0, 0, jnp.where(group == 1, 1, jnp.where(group == 2, 11, 2)))
    away = jnp.where(kind == 0, 0, jnp.where(holder == 0, 4, 8))
    origin = (z + NZ - near + away) % NZ
    slots = origin * NCORE + jnp.where(kind == 2, 1 - holder, holder)
    row = lax.broadcasted_iota(jnp.int32, (ROWS, NP), 0)
    col = lax.broadcasted_iota(jnp.int32, (ROWS, NP), 1)
    expand = ((row // MU) == col).astype(F32).astype(BF16)
    pick = lax.broadcasted_iota(jnp.int32, (NP, ROWS), 0) == slots
    pick = pick.astype(F32).astype(BF16)
    row = lax.broadcasted_iota(jnp.int32, (ROWS, ROWS), 0)
    col = lax.broadcasted_iota(jnp.int32, (ROWS, ROWS), 1)
    same = (row % MU) == (col % MU)
    dot = functools.partial(jnp.dot, preferred_element_type=F32)
    wide = [dot(dot(expand, piece).astype(BF16), pick) for piece in halves(metric.T)]
    return [jnp.where(same, piece, 0.0).astype(BF16) for piece in wide]


def stack_kernel(own_ref, got_ref, far_ref):
    far_ref[:SIG] = own_ref[...]
    far_ref[SIG:] = got_ref[...]


def stacked(own, got):
    local = pl.BlockSpec(memory_space=pltpu.VMEM)
    return pl.pallas_call(
        stack_kernel,
        in_specs=[local] * 2,
        out_specs=local,
        out_shape=jax.ShapeDtypeStruct((3 * SIG, L), F32),
        compiler_params=pltpu.CompilerParams(vmem_limit_bytes=8 * 1024 * 1024),
        cost_estimate=pl.CostEstimate(
            flops=40_000_000_000, bytes_accessed=2_000_000, transcendentals=0
        ),
    )(own, got)


def halves(a):
    top = a.astype(BF16)
    return top, (a - top.astype(F32)).astype(BF16)


def dot3(a, b):
    a_top, a_low = halves(a)
    b_top, b_low = halves(b)
    dot = functools.partial(jnp.dot, preferred_element_type=F32)
    return dot(a_top, b_top) + (dot(a_low, b_top) + dot(a_top, b_low))


def exchange_kernel(parts_ref, metric_ref, *refs):
    aux_refs, out_ref = refs[:-1], refs[-1]
    mix_top, mix_low = mixing(lax.axis_index("z"), lax.axis_index("core"), metric_ref[...])
    dot = functools.partial(jnp.dot, preferred_element_type=F32)
    coeffs = parts_ref[0]
    for y in range(1, NY):
        coeffs = coeffs + parts_ref[y]
    top, low = halves(coeffs)
    fitted = dot(top, mix_top) + (dot(low, mix_top) + dot(top, mix_low))
    fitted = fitted.T
    total = None
    for g, aux_ref in enumerate(aux_refs):
        slots = range(g * 3, (g + 1) * 3)
        left = jnp.concatenate([fitted[s * MU : (s + 1) * MU] for s in slots], axis=1)
        term = dot3(left, aux_ref[...])
        total = term if total is None else total + term
    for c in range(NY * NX):
        lane, row = (c // 4) * BLK, (c % 4) * 4
        out_ref[c] = total[row : row + 4, lane : lane + BLK]


def exchange_partial(parts, metric, aux_groups):
    local = pl.BlockSpec(memory_space=pltpu.VMEM)
    return pl.pallas_call(
        exchange_kernel,
        in_specs=[local] * (2 + len(aux_groups)),
        out_specs=local,
        out_shape=jax.ShapeDtypeStruct((NY * NX, 4, BLK), F32),
        compiler_params=pltpu.CompilerParams(vmem_limit_bytes=16 * 1024 * 1024),
        cost_estimate=pl.CostEstimate(
            flops=6 * MU * NP * SIG * L, bytes_accessed=4_000_000, transcendentals=0
        ),
    )(parts, metric, *aux_groups)


def shift(a, axis, size, by):
    return lax.ppermute(a, axis, [(i, (i + by) % size) for i in range(size)])


def on_device(three_center, density, pair_mask, metric, aux_pairs):
    own = aux_pairs.reshape(SIG, L)
    part = partial_coeffs(True, pair_mask, three_center, density)
    own, part = lax.optimization_barrier((own, part))
    both = jnp.concatenate([own, shift(own, "core", NCORE, 1)], axis=0)
    ways = [
        (z * NCORE + core, (z + (8, 4)[core]) % NZ * NCORE + core)
        for z in range(NZ)
        for core in range(NCORE)
    ]
    far = stacked(own, lax.ppermute(both, ("z", "core"), ways))
    groups = [far, *[shift(far, "z", NZ, by) for by in (1, 11, 2)]]
    groups += [shift(g, "core", NCORE, 1) for g in groups]
    part = partial_coeffs(False, pair_mask, three_center, density, part)

    got = lax.all_to_all(part, "x", 0, 0, tiled=True)
    near = summed(got)
    got = lax.all_to_all(near, "y", 0, 0, tiled=True)
    term = exchange_partial(got, metric, groups)
    got = lax.all_to_all(term, ("y", "x"), 0, 0, tiled=True)
    done = jnp.broadcast_to(jnp.sum(got, axis=0)[None], (NY * NX, 4, BLK))
    full = lax.all_to_all(done, ("y", "x"), 0, 0, tiled=True)
    return full.reshape(8, MU, BLK).transpose(1, 0, 2).reshape(MU, L)


def solution(mesh):
    grid = Mesh(mesh.devices.reshape(NZ, NCORE, NY, NX), ("z", "core", "y", "x"))
    row, col = ("z", "core"), ("y", "x")
    placed = (P(None, row, col), P(col, None), P(row, col), P(), P(row, col, None))
    return jax.shard_map(
        on_device, mesh=grid, in_specs=placed, out_specs=P(row, None), check_vma=False
    )
```

```python
import functools

import jax
import jax.numpy as jnp
from jax import lax
from jax.experimental import pallas as pl
from jax.experimental.pallas import tpu as pltpu
from jax.sharding import Mesh
from jax.sharding import PartitionSpec as P

BLK = 128
NZ, NCORE, NY, NX = 12, 2, 8, 4
NP, MU, NLOC, L = 24, 16, 4096, 1024
SIG = 32
ROWS = NP * MU
KB = 512
AHEAD = 4
F32, BF16 = jnp.float32, jnp.bfloat16


def coeff_kernel(ahead, mask_ref, three_hbm, dens_hbm, *refs):
    out_hbm, three, dens, acc, out, three_sem, dens_sem, out_sem = refs[-8:]
    z = lax.axis_index("z")

    @pl.when((z < AHEAD) if ahead else (z >= AHEAD))
    def _():
        copies = []
        for i in range(NLOC // KB):
            part = pl.ds(i * KB, KB)
            pair = (
                pltpu.make_async_copy(three_hbm.at[:, :, part], three.at[:, :, part], three_sem.at[i]),
                pltpu.make_async_copy(dens_hbm.at[part], dens.at[part], dens_sem.at[i]),
            )
            for copy in pair:
                copy.start()
            copies.append(pair)
        mask = mask_ref[...].astype(F32)
        for i, pair in enumerate(copies):
            blocks = range(i * KB // BLK, (i + 1) * KB // BLK)
            wide = [jnp.broadcast_to(mask[:, b : b + 1], (MU, BLK)) for b in blocks]
            wide = jnp.concatenate(wide, axis=1).astype(BF16)
            for copy in pair:
                copy.wait()
            masked = (three[:, :, i * KB : (i + 1) * KB] * wide[None]).reshape(ROWS, KB)
            term = jnp.dot(masked, dens[i * KB : (i + 1) * KB, :], preferred_element_type=F32)
            if i == 0:
                acc[...] = term
            elif i < len(copies) - 1:
                acc[...] += term
            else:
                total = acc[...] + term
        backs = []
        for y in range(NY):
            rows = pl.ds(y * SIG, SIG)
            turned = total[:, y * BLK : (y + 1) * BLK].T
            out[:, y * SIG : (y + 1) * SIG, :] = turned.reshape(NX, SIG, ROWS)
            back = pltpu.make_async_copy(out.at[:, rows], out_hbm.at[:, rows], out_sem.at[y])
            back.start()
            backs.append(back)
        for back in backs:
            back.wait()


def partial_coeffs(ahead, pair_mask, three_center, density, *held):
    chunks = NLOC // KB
    anywhere = pl.BlockSpec(memory_space=pl.ANY)
    part = jax.ShapeDtypeStruct((NX, NY * SIG, ROWS), F32)
    return pl.pallas_call(
        functools.partial(coeff_kernel, ahead),
        in_specs=[pl.BlockSpec(memory_space=pltpu.VMEM)] + [anywhere] * (2 + len(held)),
        out_specs=anywhere,
        out_shape=part,
        scratch_shapes=[
            pltpu.VMEM((NP, MU, NLOC), BF16),
            pltpu.VMEM((NLOC, L), BF16),
            pltpu.VMEM((ROWS, L), F32),
            pltpu.VMEM((NX, NY * SIG, ROWS), F32),
            pltpu.SemaphoreType.DMA((chunks,)),
            pltpu.SemaphoreType.DMA((chunks,)),
            pltpu.SemaphoreType.DMA((NY,)),
        ],
        input_output_aliases={} if ahead else {3: 0},
        compiler_params=pltpu.CompilerParams(vmem_limit_bytes=56 * 1024 * 1024),
        cost_estimate=pl.CostEstimate(
            flops=2 * ROWS * NLOC * L, bytes_accessed=13_000_000, transcendentals=0
        ),
    )(pair_mask, three_center, density, *held)


def sum_kernel(got_ref, out_ref):
    for y in range(NY):
        got = got_ref[:, y * SIG : (y + 1) * SIG]
        out_ref[y] = (got[0] + got[1]) + (got[2] + got[3])


def summed(got):
    return pl.pallas_call(
        sum_kernel,
        in_specs=[pl.BlockSpec(memory_space=pltpu.VMEM)],
        out_specs=pl.BlockSpec(memory_space=pltpu.VMEM),
        out_shape=jax.ShapeDtypeStruct((NY, SIG, ROWS), F32),
        compiler_params=pltpu.CompilerParams(vmem_limit_bytes=4 * 1024 * 1024),
        cost_estimate=pl.CostEstimate(
            flops=NX * NY * SIG * ROWS, bytes_accessed=2_000_000, transcendentals=0
        ),
    )(got)


def mixing(z, core, metric):
    slot = lax.broadcasted_iota(jnp.int32, (1, ROWS), 1) // MU
    holder = jnp.where(slot < NZ, core, 1 - core)
    group, kind = (slot % NZ) // 3, slot % 3
    near = jnp.where(group == 0, 0, jnp.where(group == 1, 1, jnp.where(group == 2, 11, 2)))
    away = jnp.where(kind == 0, 0, jnp.where(holder == 0, 4, 8))
    origin = (z + NZ - near + away) % NZ
    slots = origin * NCORE + jnp.where(kind == 2, 1 - holder, holder)
    row = lax.broadcasted_iota(jnp.int32, (ROWS, NP), 0)
    col = lax.broadcasted_iota(jnp.int32, (ROWS, NP), 1)
    expand = ((row // MU) == col).astype(F32).astype(BF16)
    pick = lax.broadcasted_iota(jnp.int32, (NP, ROWS), 0) == slots
    pick = pick.astype(F32).astype(BF16)
    row = lax.broadcasted_iota(jnp.int32, (ROWS, ROWS), 0)
    col = lax.broadcasted_iota(jnp.int32, (ROWS, ROWS), 1)
    same = (row % MU) == (col % MU)
    dot = functools.partial(jnp.dot, preferred_element_type=F32)
    wide = [dot(dot(expand, piece).astype(BF16), pick) for piece in halves(metric.T)]
    return [jnp.where(same, piece, 0.0).astype(BF16) for piece in wide]


def stack_kernel(own_ref, got_ref, far_ref):
    far_ref[:SIG] = own_ref[...]
    far_ref[SIG:] = got_ref[...]


def stacked(own, got):
    local = pl.BlockSpec(memory_space=pltpu.VMEM)
    return pl.pallas_call(
        stack_kernel,
        in_specs=[local] * 2,
        out_specs=local,
        out_shape=jax.ShapeDtypeStruct((3 * SIG, L), F32),
        compiler_params=pltpu.CompilerParams(vmem_limit_bytes=8 * 1024 * 1024),
        cost_estimate=pl.CostEstimate(
            flops=40_000_000_000, bytes_accessed=2_000_000, transcendentals=0
        ),
    )(own, got)


def halves(a):
    top = a.astype(BF16)
    return top, (a - top.astype(F32)).astype(BF16)


def dot3(a, b):
    a_top, a_low = halves(a)
    b_top, b_low = halves(b)
    dot = functools.partial(jnp.dot, preferred_element_type=F32)
    return dot(a_top, b_top) + (dot(a_low, b_top) + dot(a_top, b_low))


def exchange_kernel(parts_ref, metric_ref, *refs):
    aux_refs, out_ref = refs[:-1], refs[-1]
    mix_top, mix_low = mixing(lax.axis_index("z"), lax.axis_index("core"), metric_ref[...])
    dot = functools.partial(jnp.dot, preferred_element_type=F32)
    coeffs = parts_ref[0]
    for y in range(1, NY):
        coeffs = coeffs + parts_ref[y]
    top, low = halves(coeffs)
    fitted = dot(top, mix_top) + (dot(low, mix_top) + dot(top, mix_low))
    fitted = fitted.T
    total = None
    for g, aux_ref in enumerate(aux_refs):
        slots = range(g * 3, (g + 1) * 3)
        left = jnp.concatenate([fitted[s * MU : (s + 1) * MU] for s in slots], axis=1)
        term = dot3(left, aux_ref[...])
        total = term if total is None else total + term
    for c in range(NY * NX):
        lane, row = (c % 16) // 2 * BLK, (c // 16) * 8 + (c % 2) * 4
        out_ref[c] = total[row : row + 4, lane : lane + BLK]


def exchange_partial(parts, metric, aux_groups):
    local = pl.BlockSpec(memory_space=pltpu.VMEM)
    return pl.pallas_call(
        exchange_kernel,
        in_specs=[local] * (2 + len(aux_groups)),
        out_specs=local,
        out_shape=jax.ShapeDtypeStruct((NY * NX, 4, BLK), F32),
        compiler_params=pltpu.CompilerParams(vmem_limit_bytes=16 * 1024 * 1024),
        cost_estimate=pl.CostEstimate(
            flops=6 * MU * NP * SIG * L, bytes_accessed=4_000_000, transcendentals=0
        ),
    )(parts, metric, *aux_groups)


def shift(a, axis, size, by):
    return lax.ppermute(a, axis, [(i, (i + by) % size) for i in range(size)])


def on_device(three_center, density, pair_mask, metric, aux_pairs):
    own = aux_pairs.reshape(SIG, L)
    swap = shift(own, "core", NCORE, 1)
    part = partial_coeffs(True, pair_mask, three_center, density)
    own, swap, part = lax.optimization_barrier((own, swap, part))
    both = jnp.concatenate([own, swap], axis=0)
    ways = [
        (z * NCORE + core, (z + (8, 4)[core]) % NZ * NCORE + core)
        for z in range(NZ)
        for core in range(NCORE)
    ]
    far = stacked(own, lax.ppermute(both, ("z", "core"), ways))
    groups = [far, *[shift(far, "z", NZ, by) for by in (1, 11, 2)]]
    groups += [shift(g, "core", NCORE, 1) for g in groups]
    part = partial_coeffs(False, pair_mask, three_center, density, part)

    got = lax.all_to_all(part, "x", 0, 0, tiled=True)
    near = summed(got)
    got = lax.all_to_all(near, "y", 0, 0, tiled=True)
    term = exchange_partial(got, metric, groups)
    got = lax.all_to_all(term, ("y", "x"), 0, 0, tiled=True)
    done = jnp.broadcast_to(jnp.sum(got, axis=0)[None], (NY * NX, 4, BLK))
    full = lax.all_to_all(done, ("y", "x"), 0, 0, tiled=True)
    return full.reshape(2, 8, 8, BLK).transpose(0, 2, 1, 3).reshape(MU, L)


def solution(mesh):
    grid = Mesh(mesh.devices.reshape(NZ, NCORE, NY, NX), ("z", "core", "y", "x"))
    row, col = ("z", "core"), ("y", "x")
    placed = (P(None, row, col), P(col, None), P(row, col), P(), P(row, col, None))
    return jax.shard_map(
        on_device, mesh=grid, in_specs=placed, out_specs=P(row, None), check_vma=False
    )
```
